768 devices in a mesh: row: 8 (over z_lo, core), col: 96 (over y, z_hi, x).
Axes of the slice: x: 4, y: 8, z: 12 (z_hi: 3, z_lo: 4; z = z_hi * 4 + z_lo), core: 2. Of those that a mesh axis runs over, the one named last changes fastest.
Arguments:
- block_values: bfloat16 [1024, 393216], P('row', 'col'), may hold values from -6 to 6
- slot_rows: int32 [8, 12288], P('row', 'col'), may hold values from 0 to 383
- slot_cols: int32 [8, 12288], P('row', 'col'), may hold values from 0 to 31
- tile_counts: int32 [8, 96], P('row', 'col'), may hold values from 32 to 128, as said below
- prolong_blocks: bfloat16 [3072, 1024], P(('row', 'col')), may hold values from -0.75 to 0.75
- aggregate_ids: int32 [3072], P(('row', 'col')), may hold values from 0 to 1, as said below
Outputs:
- coarse_matrix: bfloat16 [24576, 24576], P('row', 'col')
The draws below stay inside these ranges and needn't reach their ends.
Inputs may be any that keep to these rules, and one draw needn't show every extreme that they name: `slot_rows`: slots of one tile may name the same block pair; their products add. `tile_counts`: slots at and beyond a tile's count are ignored; some tile is full. `aggregate_ids`: the 4 blocks of one device name each of its 2 aggregates at least once.
All inputs are finite; a program needn't handle non-finite values.
Results may differ from the reference program's by a relative error of at most 0.001.
Values may be sent and summed in bfloat16 or wider, within the bound.
No kernel may reach another device: no remote copies, remote signals or barrier semaphores. Data moves between devices by JAX's collectives and lax.ppermute only.
A program may use at most 64 MiB of HBM per device.

```python
import jax
import jax.numpy as jnp
from jax import lax

BS = 64
CB = 16
AD = 2
QD = 4
NS = 128
NF = 3072
N_ROW = 8
N_COL = 96


def draw_tile_counts(key, part):
    key = jax.random.fold_in(key, 11)
    first, second, third = jax.random.split(key, 3)
    counts = jax.random.randint(first, (N_ROW, N_COL), NS // 4, NS + 1)
    full_tile = jax.random.randint(second, (N_ROW, N_COL), 0, 4) == 0
    counts = jnp.where(full_tile, NS, counts)
    chosen = jax.random.randint(third, (), 0, N_ROW * N_COL)
    flat = counts.reshape(N_ROW * N_COL)
    flat = jnp.where(jnp.arange(N_ROW * N_COL) == chosen, NS, flat)
    return flat.reshape(N_ROW, N_COL).astype(jnp.int32)


def draw_aggregate_ids(key, part):
    key = jax.random.fold_in(key, 23)
    first, second = jax.random.split(key)
    groups = NF // QD
    within = jnp.arange(QD, dtype=jnp.int32)
    offsets = jax.random.randint(first, (groups, 1), 0, AD)
    spread = jax.random.randint(second, (groups, QD), 0, AD)
    covered = (within[None, :] + offsets) % AD
    result = jnp.where(within[None, :] < AD, covered, spread)
    return result.reshape(NF).astype(jnp.int32)


def plant(array, own_key, least, top_value):
    extent = array.shape
    place = [jax.random.randint(jax.random.fold_in(own_key, axis), (), 0, extent[axis]) for axis in range(len(extent))]
    array = array.at[tuple(place)].set(least)
    longest = extent.index(max(extent))
    place[longest] = (place[longest] + 1) % extent[longest]
    return array.at[tuple(place)].set(top_value)


def levels(own_key, extent, cuts, smallest, top_value):
    def one(dim, blocks):
        steps = jax.random.uniform(jax.random.fold_in(jax.random.fold_in(own_key, 6), dim), (blocks,), jnp.float32, smallest / len(cuts), top_value / len(cuts))
        return jnp.repeat(jnp.exp(steps), extent[dim] // blocks).reshape((-1,) + (1,) * (len(extent) - dim - 1))

    factor_of = one(*cuts[0])
    for cut in cuts[1:]:
        factor_of = factor_of * one(*cut)
    return factor_of


def scatter_about(rng, dims, scale, most, shards=(), kind=jnp.bfloat16):
    values = scale * jax.random.normal(rng, dims, jnp.float32)
    if shards:
        values = values * levels(rng, dims, shards, -0.22, 0.18)
    return jnp.clip(values, -most, most).astype(kind)


def setup_inputs(seed: int = 0) -> dict:
    streams_of = jax.random.split(jax.random.key(seed), 7)
    block_values = scatter_about(streams_of[0], (N_ROW * NS, N_COL * BS * BS), 1.0, 6.0, ((0, 8), (1, 96)))
    slot_rows = plant(jax.random.randint(streams_of[1], (N_ROW, N_COL * NS), 0, QD * N_COL), jax.random.fold_in(streams_of[1], 1), 0, (QD * N_COL) - 1).astype(jnp.int32)
    slot_cols = plant(jax.random.randint(streams_of[2], (N_ROW, N_COL * NS), 0, QD * N_ROW), jax.random.fold_in(streams_of[2], 1), 0, (QD * N_ROW) - 1).astype(jnp.int32)
    tile_counts = draw_tile_counts(jax.random.fold_in(streams_of[6], 71), 0)
    prolong_blocks = scatter_about(streams_of[4], (NF, BS * CB), BS ** -0.5, 0.75, ((0, 768),))
    aggregate_ids = draw_aggregate_ids(jax.random.fold_in(streams_of[6], 71), 0)
    return dict(block_values=block_values, slot_rows=slot_rows, slot_cols=slot_cols, tile_counts=tile_counts, prolong_blocks=prolong_blocks, aggregate_ids=aggregate_ids)


def coarse_tile(values, slot_row, slot_col, live_count, left_sel, agg_left, right_all, agg_right, row_groups, col_groups):
    blocks = values.reshape(-1, BS, BS).astype(jnp.float32)
    right_sel = right_all.reshape(-1, BS, CB)[slot_col].astype(jnp.float32)
    lefts = left_sel.reshape(-1, BS, CB).astype(jnp.float32)
    product = jnp.einsum('sxz,szy->sxy', blocks, right_sel, precision=lax.Precision.HIGHEST)
    terms = jnp.einsum('sxu,sxy->suy', lefts, product, precision=lax.Precision.HIGHEST)
    alive = (jnp.arange(slot_row.shape[0], dtype=jnp.int32) < live_count).astype(jnp.float32)
    terms = terms * alive[:, None, None]
    col_width = col_groups * AD
    target = ((slot_row // QD) * AD + agg_left) * col_width + (slot_col // QD) * AD + agg_right[slot_col]
    summed = jax.ops.segment_sum(terms, target.astype(jnp.int32), num_segments=row_groups * AD * col_width)
    summed = summed.reshape(row_groups * AD, col_width, CB, CB).transpose(0, 2, 1, 3)
    return summed.reshape(row_groups * AD * CB, col_width * CB).astype(jnp.bfloat16)


def reference(block_values, slot_rows, slot_cols, tile_counts, prolong_blocks, aggregate_ids):
    value_grid = block_values.reshape(N_ROW, NS, N_COL, BS * BS)
    row_grid = slot_rows.reshape(N_ROW, N_COL, NS)
    col_grid = slot_cols.reshape(N_ROW, N_COL, NS)
    factor_grid = prolong_blocks.reshape(N_ROW, N_COL, QD, BS * CB)
    agg_grid = aggregate_ids.reshape(N_ROW, N_COL, QD)

    def one_tile(position):
        row_at = position // N_COL
        col_at = position % N_COL
        values = value_grid[row_at, :, col_at]
        slot_row = row_grid[row_at, col_at]
        slot_col = col_grid[row_at, col_at]
        slab_factor = factor_grid[row_at].reshape(N_COL * QD, BS * CB)
        slab_agg = agg_grid[row_at].reshape(N_COL * QD)
        column_factor = factor_grid[:, col_at].reshape(N_ROW * QD, BS * CB)
        column_agg = agg_grid[:, col_at].reshape(N_ROW * QD)
        return coarse_tile(values, slot_row, slot_col, tile_counts[row_at, col_at], slab_factor[slot_row], slab_agg[slot_row], column_factor, column_agg, N_COL, N_ROW)

    pieces = lax.map(one_tile, jnp.arange(N_ROW * N_COL, dtype=jnp.int32))
    height = pieces.shape[1]
    breadth = pieces.shape[2]
    return pieces.reshape(N_ROW, N_COL, height, breadth).transpose(0, 2, 1, 3).reshape(N_ROW * height, N_COL * breadth)
```

```python
import jax
import jax.numpy as jnp
from jax import lax
from jax.experimental import pallas as pl
from jax.experimental.pallas import tpu as pltpu
from jax.sharding import PartitionSpec as P

BS = 64
CB = 16
AD = 2
QD = 4
NEAR = 4
DEEP = 3
LANES = 128
PARTS = 2
CHUNKS = 6
WIDE = BS * CB + LANES


def hot_slots(index, blocks):
    slots = index.shape[1]
    hot = lax.broadcasted_iota(jnp.int32, (blocks, slots), 0) == index
    return hot.astype(jnp.float32).T.astype(jnp.bfloat16)


def slots_to_lanes(picked, target):
    for k in range(WIDE // LANES):
        target[pl.ds(k * LANES, LANES), :] = picked[:, k * LANES:(k + 1) * LANES].T


def right_kernel(me_ref, a_ref, held_ref, rest_ref, row_ref, col_ref, z_ref, coarse_ref, pick_ref, at, rt):
    f32 = jnp.float32
    slots = a_ref.shape[0]
    slot_col = col_ref[...]
    half = held_ref.shape[0]
    place = ((slot_col >> 2) ^ me_ref[0, 0]) * QD + (slot_col & (QD - 1))
    picked = jnp.dot(hot_slots(place, half), held_ref[...], preferred_element_type=f32)
    picked += jnp.dot(hot_slots(place - half, half), rest_ref[...], preferred_element_type=f32)
    slots_to_lanes(picked, rt)
    for k in range(BS * BS // LANES):
        at[pl.ds(k * LANES, LANES), :] = a_ref[:, k * LANES:(k + 1) * LANES].astype(f32).T

    group = 8

    def x_block(b, carry):
        base = pl.multiple_of(b * (group * BS), group * BS)
        sums = [jnp.zeros((CB, slots), f32) for _ in range(group)]
        for z in range(BS):
            r = rt[pl.ds(z * CB, CB), :]
            for xi in range(group):
                sums[xi] = sums[xi] + at[pl.ds(base + (xi * BS + z), 1), :] * r
        for xi in range(group):
            z_ref[pl.ds(pl.multiple_of(b * (group * CB), group * CB) + xi * CB, CB), :] = sums[xi]
        return carry

    lax.fori_loop(0, BS // group, x_block, 0)
    coarse_ref[...] = (slot_col >> 2) * AD + rt[pl.ds(BS * CB, 1), :].astype(jnp.int32)
    slot_row = row_ref[...]
    device = slot_row >> 2
    blocks = pick_ref.shape[1]
    place = (device & (NEAR - 1)) * (blocks // NEAR) + (device >> 2) * QD + (slot_row & (QD - 1))
    pick_ref[...] = hot_slots(place, blocks)


def left_kernel(count_ref, left_ref, pick_ref, z_ref, coarse_ref, row_ref, out_ref, lt, acc0, acc1, staged, sems):
    f32 = jnp.float32
    bf16 = jnp.bfloat16
    slots = z_ref.shape[1]
    slots_to_lanes(jnp.dot(pick_ref[...], left_ref[...], preferred_element_type=f32), lt)

    def x_step(b, sums):
        base = pl.multiple_of(b * (4 * CB), 4 * CB)
        sums = list(sums)
        for xi in range(4):
            zx = z_ref[pl.ds(base + xi * CB, CB), :]
            for u in range(CB):
                sums[u] = sums[u] + lt[pl.ds(base + (xi * CB + u), 1), :] * zx
        return tuple(sums)

    terms = lax.fori_loop(0, BS // 4, x_step, tuple(jnp.zeros((CB, slots), f32) for _ in range(CB)))

    coarse_row = (row_ref[...] >> 2) * AD + lt[pl.ds(BS * CB, 1), :].astype(jnp.int32)
    live = lax.broadcasted_iota(jnp.int32, (1, slots), 1) < count_ref[0, 0]
    coarse_row = jnp.where(live, coarse_row, -1)
    coarse_col = coarse_ref[...]
    rows = out_ref.shape[0] // CB
    cols = out_ref.shape[1] // CB
    hot = (lax.broadcasted_iota(jnp.int32, (rows, slots), 0) == coarse_row).astype(bf16)
    hot = jnp.concatenate([hot] * PARTS, axis=1)
    masks = [jnp.broadcast_to((coarse_col == v).astype(f32), (CB, slots)).astype(bf16) for v in range(cols)]

    for u in range(CB):
        rest = terms[u]
        placed = []
        for _ in range(PARTS):
            part = rest.astype(bf16)
            rest = rest - part.astype(f32)
            placed.append(jnp.concatenate([mask * part for mask in masks], axis=0))
        placed = jnp.concatenate(placed, axis=1)
        summed = lax.dot_general(hot, placed, (((1,), (1,)), ((), ())), preferred_element_type=f32)
        acc0[pl.ds(u, rows, stride=CB), :] = summed[:, :LANES]
        acc1[pl.ds(u, rows, stride=CB), :] = summed[:, LANES:]

    copies = []
    chunk = out_ref.shape[0] // CHUNKS
    for k in range(CHUNKS):
        part = pl.ds(k * chunk, chunk)
        staged[part, :LANES] = acc0[part, :].astype(bf16)
        staged[part, LANES:] = acc1[part, :].astype(bf16)
        copies.append(pltpu.make_async_copy(staged.at[part, :], out_ref.at[part, :], sems.at[k]))
        copies[-1].start()
    for copy in copies:
        copy.wait()


def right_products(me, values, held, rest, slot_row, slot_col, blocks):
    slots = values.shape[0]
    f32 = jnp.float32
    vmem = pl.BlockSpec(memory_space=pltpu.VMEM)
    return pl.pallas_call(
        right_kernel,
        out_shape=[
            jax.ShapeDtypeStruct((BS * CB, slots), f32),
            jax.ShapeDtypeStruct((1, slots), jnp.int32),
            jax.ShapeDtypeStruct((slots, blocks), jnp.bfloat16),
        ],
        in_specs=[pl.BlockSpec(memory_space=pltpu.SMEM)] + [vmem] * 5,
        out_specs=[vmem] * 3,
        scratch_shapes=[pltpu.VMEM((BS * BS, slots), f32), pltpu.VMEM((WIDE, slots), f32)],
        compiler_params=pltpu.CompilerParams(vmem_limit_bytes=24 * 1024 * 1024),
    )(me, values, held, rest, slot_row, slot_col)


def coarse_tile(live_count, left, pick, z, coarse_col, slot_row, rows, cols):
    slots = z.shape[1]
    f32 = jnp.float32
    vmem = pl.BlockSpec(memory_space=pltpu.VMEM)
    return pl.pallas_call(
        left_kernel,
        out_shape=jax.ShapeDtypeStruct((rows, cols), jnp.bfloat16),
        in_specs=[pl.BlockSpec(memory_space=pltpu.SMEM)] + [vmem] * 5,
        out_specs=pl.BlockSpec(memory_space=pl.ANY),
        scratch_shapes=[
            pltpu.VMEM((WIDE, slots), f32),
            pltpu.VMEM((rows, LANES), f32),
            pltpu.VMEM((rows, LANES), f32),
            pltpu.VMEM((rows, cols), jnp.bfloat16),
            pltpu.SemaphoreType.DMA((CHUNKS,)),
        ],
        compiler_params=pltpu.CompilerParams(vmem_limit_bytes=24 * 1024 * 1024),
    )(live_count, left, pick, z, coarse_col, slot_row)


def everywhere(block, axis, size, groups=None):
    copies = jnp.broadcast_to(block[None], (size,) + block.shape)
    return lax.all_to_all(copies, axis, 0, 0, axis_index_groups=groups, tiled=True)


def shards(block_values, slot_rows, slot_cols, tile_counts, prolong_blocks, aggregate_ids):
    row_size = lax.axis_size("row")
    col_size = lax.axis_size("col")
    planes = col_size // NEAR
    ids = jnp.broadcast_to(aggregate_ids.astype(jnp.bfloat16)[:, None], (QD, LANES))
    mine = jnp.concatenate([prolong_blocks, ids], axis=1)
    held = mine[None]
    step = 1
    while 2 * step < row_size:
        held = jnp.concatenate([held, lax.ppermute(held, "row", [(r ^ step, r) for r in range(row_size)])], axis=0)
        step *= 2
    rest = lax.ppermute(held, "row", [(r ^ step, r) for r in range(row_size)])
    held = held.reshape(step * QD, WIDE)
    rest = rest.reshape(step * QD, WIDE)
    me = lax.axis_index("row").astype(jnp.int32).reshape(1, 1)
    tall = planes // DEEP
    z_groups = [[(y * DEEP + z) * NEAR + x for z in range(DEEP)] for y in range(tall) for x in range(NEAR)]
    y_groups = [[(y * DEEP + z) * NEAR + x for y in range(tall)] for z in range(DEEP) for x in range(NEAR)]
    x_groups = [[p * NEAR + x for x in range(NEAR)] for p in range(planes)]
    line = everywhere(mine, "col", DEEP, z_groups)
    plane = everywhere(line, "col", tall, y_groups).reshape(planes * QD, WIDE)
    plane, held = lax.optimization_barrier((plane, held))
    left = everywhere(plane, "col", NEAR, x_groups).reshape(col_size * QD, WIDE)
    z, coarse_col, pick = right_products(me, block_values, held, rest, slot_rows, slot_cols, col_size * QD)
    return coarse_tile(
        tile_counts, left, pick, z, coarse_col, slot_rows, col_size * AD * CB, row_size * AD * CB
    )


def solution(mesh):
    placed = (
        P("row", "col"),
        P("row", "col"),
        P("row", "col"),
        P("row", "col"),
        P(("row", "col"), None),
        P(("row", "col")),
    )
    return jax.shard_map(
        shards, mesh=mesh, in_specs=placed, out_specs=P("row", "col"), check_vma=False
    )
```

```python
import jax
import jax.numpy as jnp
from jax import lax
from jax.experimental import pallas as pl
from jax.experimental.pallas import tpu as pltpu
from jax.sharding import PartitionSpec as P

BS = 64
CB = 16
AD = 2
QD = 4
NEAR = 4
LANES = 128
PARTS = 2
CHUNKS = 6
WIDE = BS * CB + LANES


def hot_slots(index, blocks):
    slots = index.shape[1]
    hot = lax.broadcasted_iota(jnp.int32, (blocks, slots), 0) == index
    return hot.astype(jnp.float32).T.astype(jnp.bfloat16)


def slots_to_lanes(picked, target):
    for k in range(WIDE // LANES):
        target[pl.ds(k * LANES, LANES), :] = picked[:, k * LANES:(k + 1) * LANES].T


def right_kernel(me_ref, a_ref, held_ref, rest_ref, row_ref, col_ref, z_ref, coarse_ref, pick_ref, at, rt):
    f32 = jnp.float32
    slots = a_ref.shape[0]
    slot_col = col_ref[...]
    half = held_ref.shape[0]
    place = ((slot_col >> 2) ^ me_ref[0, 0]) * QD + (slot_col & (QD - 1))
    picked = jnp.dot(hot_slots(place, half), held_ref[...], preferred_element_type=f32)
    picked += jnp.dot(hot_slots(place - half, half), rest_ref[...], preferred_element_type=f32)
    slots_to_lanes(picked, rt)
    for k in range(BS * BS // LANES):
        at[pl.ds(k * LANES, LANES), :] = a_ref[:, k * LANES:(k + 1) * LANES].astype(f32).T

    group = 8

    def x_block(b, carry):
        base = pl.multiple_of(b * (group * BS), group * BS)
        sums = [jnp.zeros((CB, slots), f32) for _ in range(group)]
        for z in range(BS):
            r = rt[pl.ds(z * CB, CB), :]
            for xi in range(group):
                sums[xi] = sums[xi] + at[pl.ds(base + (xi * BS + z), 1), :] * r
        for xi in range(group):
            z_ref[pl.ds(pl.multiple_of(b * (group * CB), group * CB) + xi * CB, CB), :] = sums[xi]
        return carry

    lax.fori_loop(0, BS // group, x_block, 0)
    coarse_ref[...] = (slot_col >> 2) * AD + rt[pl.ds(BS * CB, 1), :].astype(jnp.int32)
    slot_row = row_ref[...]
    device = slot_row >> 2
    blocks = pick_ref.shape[1]
    place = (device & (NEAR - 1)) * (blocks // NEAR) + (device >> 2) * QD + (slot_row & (QD - 1))
    pick_ref[...] = hot_slots(place, blocks)


def left_kernel(count_ref, left_ref, pick_ref, z_ref, coarse_ref, row_ref, out_ref, lt, acc0, acc1, staged, sems):
    f32 = jnp.float32
    bf16 = jnp.bfloat16
    slots = z_ref.shape[1]
    slots_to_lanes(jnp.dot(pick_ref[...], left_ref[...], preferred_element_type=f32), lt)

    def x_step(b, sums):
        base = pl.multiple_of(b * (8 * CB), 8 * CB)
        sums = list(sums)
        for xi in range(8):
            zx = z_ref[pl.ds(base + xi * CB, CB), :]
            for u in range(CB):
                sums[u] = sums[u] + lt[pl.ds(base + (xi * CB + u), 1), :] * zx
        return tuple(sums)

    terms = lax.fori_loop(0, BS // 8, x_step, tuple(jnp.zeros((CB, slots), f32) for _ in range(CB)))

    coarse_row = (row_ref[...] >> 2) * AD + lt[pl.ds(BS * CB, 1), :].astype(jnp.int32)
    live = lax.broadcasted_iota(jnp.int32, (1, slots), 1) < count_ref[0, 0]
    coarse_row = jnp.where(live, coarse_row, -1)
    coarse_col = coarse_ref[...]
    rows = out_ref.shape[0] // CB
    cols = out_ref.shape[1] // CB
    hot = (lax.broadcasted_iota(jnp.int32, (rows, slots), 0) == coarse_row).astype(bf16)
    hot = jnp.concatenate([hot] * PARTS, axis=1)
    masks = [jnp.broadcast_to((coarse_col == v).astype(f32), (CB, slots)).astype(bf16) for v in range(cols)]

    for u in range(CB):
        rest = terms[u]
        placed = []
        for _ in range(PARTS):
            part = rest.astype(bf16)
            rest = rest - part.astype(f32)
            placed.append(jnp.concatenate([mask * part for mask in masks], axis=0))
        placed = jnp.concatenate(placed, axis=1)
        summed = lax.dot_general(hot, placed, (((1,), (1,)), ((), ())), preferred_element_type=f32)
        acc0[pl.ds(u, rows, stride=CB), :] = summed[:, :LANES]
        acc1[pl.ds(u, rows, stride=CB), :] = summed[:, LANES:]

    copies = []
    chunk = out_ref.shape[0] // CHUNKS
    for k in range(CHUNKS):
        part = pl.ds(k * chunk, chunk)
        staged[part, :LANES] = acc0[part, :].astype(bf16)
        staged[part, LANES:] = acc1[part, :].astype(bf16)
        copies.append(pltpu.make_async_copy(staged.at[part, :], out_ref.at[part, :], sems.at[k]))
        copies[-1].start()
    for copy in copies:
        copy.wait()


def right_products(me, values, held, rest, slot_row, slot_col, blocks):
    slots = values.shape[0]
    f32 = jnp.float32
    vmem = pl.BlockSpec(memory_space=pltpu.VMEM)
    return pl.pallas_call(
        right_kernel,
        out_shape=[
            jax.ShapeDtypeStruct((BS * CB, slots), f32),
            jax.ShapeDtypeStruct((1, slots), jnp.int32),
            jax.ShapeDtypeStruct((slots, blocks), jnp.bfloat16),
        ],
        in_specs=[pl.BlockSpec(memory_space=pltpu.SMEM)] + [vmem] * 5,
        out_specs=[vmem] * 3,
        scratch_shapes=[pltpu.VMEM((BS * BS, slots), f32), pltpu.VMEM((WIDE, slots), f32)],
        compiler_params=pltpu.CompilerParams(vmem_limit_bytes=24 * 1024 * 1024),
    )(me, values, held, rest, slot_row, slot_col)


def coarse_tile(live_count, left, pick, z, coarse_col, slot_row, rows, cols):
    slots = z.shape[1]
    f32 = jnp.float32
    vmem = pl.BlockSpec(memory_space=pltpu.VMEM)
    return pl.pallas_call(
        left_kernel,
        out_shape=jax.ShapeDtypeStruct((rows, cols), jnp.bfloat16),
        in_specs=[pl.BlockSpec(memory_space=pltpu.SMEM)] + [vmem] * 5,
        out_specs=pl.BlockSpec(memory_space=pl.ANY),
        scratch_shapes=[
            pltpu.VMEM((WIDE, slots), f32),
            pltpu.VMEM((rows, LANES), f32),
            pltpu.VMEM((rows, LANES), f32),
            pltpu.VMEM((rows, cols), jnp.bfloat16),
            pltpu.SemaphoreType.DMA((CHUNKS,)),
        ],
        compiler_params=pltpu.CompilerParams(vmem_limit_bytes=24 * 1024 * 1024),
    )(live_count, left, pick, z, coarse_col, slot_row)


def payload_kernel(ids_ref, blocks_ref, copies_ref):
    row = lax.broadcasted_iota(jnp.int32, (QD, LANES), 0)
    ids = jnp.zeros((QD, LANES), jnp.float32)
    for t in range(QD):
        ids = jnp.where(row == t, ids_ref[t].astype(jnp.float32), ids)
    whole = jnp.concatenate([blocks_ref[...].astype(jnp.float32), ids], axis=1).astype(jnp.bfloat16)
    for k in range(copies_ref.shape[0]):
        copies_ref[k] = whole


def payload(blocks, ids, count):
    vmem = pl.BlockSpec(memory_space=pltpu.VMEM)
    return pl.pallas_call(
        payload_kernel,
        out_shape=jax.ShapeDtypeStruct((count, QD, WIDE), jnp.bfloat16),
        in_specs=[pl.BlockSpec(memory_space=pltpu.SMEM), vmem],
        out_specs=vmem,
    )(ids, blocks)


def everywhere(block, axis, size, groups=None):
    copies = jnp.broadcast_to(block[None], (size,) + block.shape)
    return lax.all_to_all(copies, axis, 0, 0, axis_index_groups=groups, tiled=True)


def shards(block_values, slot_rows, slot_cols, tile_counts, prolong_blocks, aggregate_ids):
    row_size = lax.axis_size("row")
    col_size = lax.axis_size("col")
    planes = col_size // NEAR
    copies = payload(prolong_blocks, aggregate_ids, planes)
    held = copies[:1]
    step = 1
    while 2 * step < row_size:
        held = jnp.concatenate([held, lax.ppermute(held, "row", [(r ^ step, r) for r in range(row_size)])], axis=0)
        step *= 2
    rest = lax.ppermute(held, "row", [(r ^ step, r) for r in range(row_size)])
    held = held.reshape(step * QD, WIDE)
    rest = rest.reshape(step * QD, WIDE)
    me = lax.axis_index("row").astype(jnp.int32).reshape(1, 1)
    yz_groups = [[p * NEAR + x for p in range(planes)] for x in range(NEAR)]
    x_groups = [[p * NEAR + x for x in range(NEAR)] for p in range(planes)]
    plane = lax.all_to_all(copies, "col", 0, 0, axis_index_groups=yz_groups, tiled=True).reshape(planes * QD, WIDE)
    plane, held = lax.optimization_barrier((plane, held))
    left = everywhere(plane, "col", NEAR, x_groups).reshape(col_size * QD, WIDE)
    z, coarse_col, pick = right_products(me, block_values, held, rest, slot_rows, slot_cols, col_size * QD)
    return coarse_tile(
        tile_counts, left, pick, z, coarse_col, slot_rows, col_size * AD * CB, row_size * AD * CB
    )


def solution(mesh):
    placed = (
        P("row", "col"),
        P("row", "col"),
        P("row", "col"),
        P("row", "col"),
        P(("row", "col"), None),
        P(("row", "col")),
    )
    return jax.shard_map(
        shards, mesh=mesh, in_specs=placed, out_specs=P("row", "col"), check_vma=False
    )
```

```python
import jax
import jax.numpy as jnp
from jax import lax
from jax.experimental import pallas as pl
from jax.experimental.pallas import tpu as pltpu
from jax.sharding import PartitionSpec as P

BS = 64
CB = 16
AD = 2
QD = 4
NEAR = 4
LANES = 128
PARTS = 2
CHUNKS = 6
WIDE = BS * CB + LANES


def hot_slots(index, blocks):
    slots = index.shape[1]
    hot = lax.broadcasted_iota(jnp.int32, (blocks, slots), 0) == index
    return hot.astype(jnp.float32).T.astype(jnp.bfloat16)


def slots_to_lanes(picked, target):
    for k in range(WIDE // LANES):
        target[pl.ds(k * LANES, LANES), :] = picked[:, k * LANES:(k + 1) * LANES].T


def right_kernel(me_ref, a_ref, held_ref, rest_ref, row_ref, col_ref, z_ref, coarse_ref, pick_ref, at, rt):
    f32 = jnp.float32
    slots = a_ref.shape[0]
    slot_col = col_ref[...]
    half = held_ref.shape[0]
    place = ((slot_col >> 2) ^ me_ref[0, 0]) * QD + (slot_col & (QD - 1))
    picked = jnp.dot(hot_slots(place, half), held_ref[...], preferred_element_type=f32)
    picked += jnp.dot(hot_slots(place - half, half), rest_ref[...], preferred_element_type=f32)
    slots_to_lanes(picked, rt)
    for k in range(BS * BS // LANES):
        at[pl.ds(k * LANES, LANES), :] = a_ref[:, k * LANES:(k + 1) * LANES].astype(f32).T

    group = 8

    def x_block(b, carry):
        base = pl.multiple_of(b * (group * BS), group * BS)
        sums = [jnp.zeros((CB, slots), f32) for _ in range(group)]
        for z in range(BS):
            r = rt[pl.ds(z * CB, CB), :]
            for xi in range(group):
                sums[xi] = sums[xi] + at[pl.ds(base + (xi * BS + z), 1), :] * r
        for xi in range(group):
            z_ref[pl.ds(pl.multiple_of(b * (group * CB), group * CB) + xi * CB, CB), :] = sums[xi]
        return carry

    lax.fori_loop(0, BS // group, x_block, 0)
    coarse_ref[...] = (slot_col >> 2) * AD + rt[pl.ds(BS * CB, 1), :].astype(jnp.int32)
    slot_row = row_ref[...]
    device = slot_row >> 2
    blocks = pick_ref.shape[1]
    place = (device & (NEAR - 1)) * (blocks // NEAR) + (device >> 2) * QD + (slot_row & (QD - 1))
    pick_ref[...] = hot_slots(place, blocks)


def left_kernel(count_ref, left_ref, pick_ref, z_ref, coarse_ref, row_ref, out_ref, lt, acc0, acc1, staged, sems):
    f32 = jnp.float32
    bf16 = jnp.bfloat16
    slots = z_ref.shape[1]
    slots_to_lanes(jnp.dot(pick_ref[...], left_ref[...], preferred_element_type=f32), lt)

    def x_step(b, sums):
        base = pl.multiple_of(b * (8 * CB), 8 * CB)
        sums = list(sums)
        for xi in range(8):
            zx = z_ref[pl.ds(base + xi * CB, CB), :]
            for u in range(CB):
                sums[u] = sums[u] + lt[pl.ds(base + (xi * CB + u), 1), :] * zx
        return tuple(sums)

    terms = lax.fori_loop(0, BS // 8, x_step, tuple(jnp.zeros((CB, slots), f32) for _ in range(CB)))

    coarse_row = (row_ref[...] >> 2) * AD + lt[pl.ds(BS * CB, 1), :].astype(jnp.int32)
    live = lax.broadcasted_iota(jnp.int32, (1, slots), 1) < count_ref[0, 0]
    coarse_row = jnp.where(live, coarse_row, -1)
    coarse_col = coarse_ref[...]
    rows = out_ref.shape[0] // CB
    cols = out_ref.shape[1] // CB
    hot = (lax.broadcasted_iota(jnp.int32, (rows, slots), 0) == coarse_row).astype(bf16)
    hot = jnp.concatenate([hot] * PARTS, axis=1)
    masks = [jnp.broadcast_to((coarse_col == v).astype(f32), (CB, slots)).astype(bf16) for v in range(cols)]

    for u in range(CB):
        rest = terms[u]
        placed = []
        for _ in range(PARTS):
            part = rest.astype(bf16)
            rest = rest - part.astype(f32)
            placed.append(jnp.concatenate([mask * part for mask in masks], axis=0))
        placed = jnp.concatenate(placed, axis=1)
        summed = lax.dot_general(hot, placed, (((1,), (1,)), ((), ())), preferred_element_type=f32)
        acc0[pl.ds(u, rows, stride=CB), :] = summed[:, :LANES]
        acc1[pl.ds(u, rows, stride=CB), :] = summed[:, LANES:]

    copies = []
    chunk = out_ref.shape[0] // CHUNKS
    for k in range(CHUNKS):
        part = pl.ds(k * chunk, chunk)
        staged[part, :LANES] = acc0[part, :].astype(bf16)
        staged[part, LANES:] = acc1[part, :].astype(bf16)
        copies.append(pltpu.make_async_copy(staged.at[part, :], out_ref.at[part, :], sems.at[k]))
        copies[-1].start()
    for copy in copies:
        copy.wait()


def right_products(me, values, held, rest, slot_row, slot_col, blocks):
    slots = values.shape[0]
    f32 = jnp.float32
    vmem = pl.BlockSpec(memory_space=pltpu.VMEM)
    return pl.pallas_call(
        right_kernel,
        out_shape=[
            jax.ShapeDtypeStruct((BS * CB, slots), f32),
            jax.ShapeDtypeStruct((1, slots), jnp.int32),
            jax.ShapeDtypeStruct((slots, blocks), jnp.bfloat16),
        ],
        in_specs=[pl.BlockSpec(memory_space=pltpu.SMEM)] + [vmem] * 5,
        out_specs=[vmem] * 3,
        scratch_shapes=[pltpu.VMEM((BS * BS, slots), f32), pltpu.VMEM((WIDE, slots), f32)],
        compiler_params=pltpu.CompilerParams(vmem_limit_bytes=24 * 1024 * 1024),
    )(me, values, held, rest, slot_row, slot_col)


def coarse_tile(live_count, left, pick, z, coarse_col, slot_row, rows, cols):
    slots = z.shape[1]
    f32 = jnp.float32
    vmem = pl.BlockSpec(memory_space=pltpu.VMEM)
    return pl.pallas_call(
        left_kernel,
        out_shape=jax.ShapeDtypeStruct((rows, cols), jnp.bfloat16),
        in_specs=[pl.BlockSpec(memory_space=pltpu.SMEM)] + [vmem] * 5,
        out_specs=pl.BlockSpec(memory_space=pl.ANY),
        scratch_shapes=[
            pltpu.VMEM((WIDE, slots), f32),
            pltpu.VMEM((rows, LANES), f32),
            pltpu.VMEM((rows, LANES), f32),
            pltpu.VMEM((rows, cols), jnp.bfloat16),
            pltpu.SemaphoreType.DMA((CHUNKS,)),
        ],
        compiler_params=pltpu.CompilerParams(vmem_limit_bytes=24 * 1024 * 1024),
    )(live_count, left, pick, z, coarse_col, slot_row)


def payload_kernel(ids_ref, blocks_ref, mine_ref, copies_ref):
    row = lax.broadcasted_iota(jnp.int32, (QD, LANES), 0)
    ids = jnp.zeros((QD, LANES), jnp.float32)
    for t in range(QD):
        ids = jnp.where(row == t, ids_ref[t].astype(jnp.float32), ids)
    whole = jnp.concatenate([blocks_ref[...].astype(jnp.float32), ids], axis=1).astype(jnp.bfloat16)
    mine_ref[0] = whole
    for k in range(copies_ref.shape[0]):
        copies_ref[k] = whole


def payload(blocks, ids, count):
    vmem = pl.BlockSpec(memory_space=pltpu.VMEM)
    return pl.pallas_call(
        payload_kernel,
        out_shape=[
            pltpu.VMEM((1, QD, WIDE), jnp.bfloat16),
            jax.ShapeDtypeStruct((count, QD, WIDE), jnp.bfloat16),
        ],
        in_specs=[pl.BlockSpec(memory_space=pltpu.SMEM), vmem],
        out_specs=[vmem, vmem],
    )(ids, blocks)


def everywhere(block, axis, size, groups=None):
    copies = jnp.broadcast_to(block[None], (size,) + block.shape)
    return lax.all_to_all(copies, axis, 0, 0, axis_index_groups=groups, tiled=True)


def shards(block_values, slot_rows, slot_cols, tile_counts, prolong_blocks, aggregate_ids):
    row_size = lax.axis_size("row")
    col_size = lax.axis_size("col")
    planes = col_size // NEAR
    mine, copies = payload(prolong_blocks, aggregate_ids, planes)
    held = mine
    step = 1
    while 2 * step < row_size:
        held = jnp.concatenate([held, lax.ppermute(held, "row", [(r ^ step, r) for r in range(row_size)])], axis=0)
        step *= 2
    rest = lax.ppermute(held, "row", [(r ^ step, r) for r in range(row_size)])
    held = held.reshape(step * QD, WIDE)
    rest = rest.reshape(step * QD, WIDE)
    me = lax.axis_index("row").astype(jnp.int32).reshape(1, 1)
    yz_groups = [[p * NEAR + x for p in range(planes)] for x in range(NEAR)]
    x_groups = [[p * NEAR + x for x in range(NEAR)] for p in range(planes)]
    plane = lax.all_to_all(copies, "col", 0, 0, axis_index_groups=yz_groups, tiled=True).reshape(planes * QD, WIDE)
    plane, held = lax.optimization_barrier((plane, held))
    left = everywhere(plane, "col", NEAR, x_groups).reshape(col_size * QD, WIDE)
    z, coarse_col, pick = right_products(me, block_values, held, rest, slot_rows, slot_cols, col_size * QD)
    return coarse_tile(
        tile_counts, left, pick, z, coarse_col, slot_rows, col_size * AD * CB, row_size * AD * CB
    )


def solution(mesh):
    placed = (
        P("row", "col"),
        P("row", "col"),
        P("row", "col"),
        P("row", "col"),
        P(("row", "col"), None),
        P(("row", "col")),
    )
    return jax.shard_map(
        shards, mesh=mesh, in_specs=placed, out_specs=P("row", "col"), check_vma=False
    )
```

```python
import jax
import jax.numpy as jnp
from jax import lax
from jax.experimental import pallas as pl
from jax.experimental.pallas import tpu as pltpu
from jax.sharding import PartitionSpec as P

BS = 64
CB = 16
AD = 2
QD = 4
NEAR = 4
LANES = 128
PARTS = 2
CHUNKS = 6
WIDE = BS * CB + LANES


def hot_slots(index, blocks):
    slots = index.shape[1]
    hot = lax.broadcasted_iota(jnp.int32, (blocks, slots), 0) == index
    return hot.astype(jnp.float32).T.astype(jnp.bfloat16)


def slots_to_lanes(picked, target):
    for k in range(WIDE // LANES):
        target[pl.ds(k * LANES, LANES), :] = picked[:, k * LANES:(k + 1) * LANES].T


def right_kernel(me_ref, a_ref, held_ref, rest_ref, row_ref, col_ref, z_ref, coarse_ref, pick_ref, at, rt):
    f32 = jnp.float32
    slots = a_ref.shape[0]
    slot_col = col_ref[...]
    half = held_ref.shape[0]
    away = (slot_col >> 2) ^ me_ref[0, 0]
    turned = ((away & 1) << 2) | (away & 2) | (away >> 2)
    place = turned * QD + (slot_col & (QD - 1))
    picked = jnp.dot(hot_slots(place, half), held_ref[...], preferred_element_type=f32)
    picked += jnp.dot(hot_slots(place - half, half), rest_ref[...], preferred_element_type=f32)
    slots_to_lanes(picked, rt)
    for k in range(BS * BS // LANES):
        at[pl.ds(k * LANES, LANES), :] = a_ref[:, k * LANES:(k + 1) * LANES].astype(f32).T

    group = 8

    def x_block(b, carry):
        base = pl.multiple_of(b * (group * BS), group * BS)
        sums = [jnp.zeros((CB, slots), f32) for _ in range(group)]
        for z in range(BS):
            r = rt[pl.ds(z * CB, CB), :]
            for xi in range(group):
                sums[xi] = sums[xi] + at[pl.ds(base + (xi * BS + z), 1), :] * r
        for xi in range(group):
            z_ref[pl.ds(pl.multiple_of(b * (group * CB), group * CB) + xi * CB, CB), :] = sums[xi]
        return carry

    lax.fori_loop(0, BS // group, x_block, 0)
    coarse_ref[...] = (slot_col >> 2) * AD + rt[pl.ds(BS * CB, 1), :].astype(jnp.int32)
    slot_row = row_ref[...]
    device = slot_row >> 2
    blocks = pick_ref.shape[1]
    place = (device & (NEAR - 1)) * (blocks // NEAR) + (device >> 2) * QD + (slot_row & (QD - 1))
    pick_ref[...] = hot_slots(place, blocks)


def left_kernel(count_ref, left_ref, pick_ref, z_ref, coarse_ref, row_ref, out_ref, lt, acc0, acc1, staged, sems):
    f32 = jnp.float32
    bf16 = jnp.bfloat16
    slots = z_ref.shape[1]
    slots_to_lanes(jnp.dot(pick_ref[...], left_ref[...], preferred_element_type=f32), lt)

    def x_step(b, sums):
        base = pl.multiple_of(b * (8 * CB), 8 * CB)
        sums = list(sums)
        for xi in range(8):
            zx = z_ref[pl.ds(base + xi * CB, CB), :]
            for u in range(CB):
                sums[u] = sums[u] + lt[pl.ds(base + (xi * CB + u), 1), :] * zx
        return tuple(sums)

    terms = lax.fori_loop(0, BS // 8, x_step, tuple(jnp.zeros((CB, slots), f32) for _ in range(CB)))

    coarse_row = (row_ref[...] >> 2) * AD + lt[pl.ds(BS * CB, 1), :].astype(jnp.int32)
    live = lax.broadcasted_iota(jnp.int32, (1, slots), 1) < count_ref[0, 0]
    coarse_row = jnp.where(live, coarse_row, -1)
    coarse_col = coarse_ref[...]
    rows = out_ref.shape[0] // CB
    cols = out_ref.shape[1] // CB
    hot = (lax.broadcasted_iota(jnp.int32, (rows, slots), 0) == coarse_row).astype(bf16)
    hot = jnp.concatenate([hot] * PARTS, axis=1)
    masks = [jnp.broadcast_to((coarse_col == v).astype(f32), (CB, slots)).astype(bf16) for v in range(cols)]

    for u in range(CB):
        rest = terms[u]
        placed = []
        for _ in range(PARTS):
            part = rest.astype(bf16)
            rest = rest - part.astype(f32)
            placed.append(jnp.concatenate([mask * part for mask in masks], axis=0))
        placed = jnp.concatenate(placed, axis=1)
        summed = lax.dot_general(hot, placed, (((1,), (1,)), ((), ())), preferred_element_type=f32)
        acc0[pl.ds(u, rows, stride=CB), :] = summed[:, :LANES]
        acc1[pl.ds(u, rows, stride=CB), :] = summed[:, LANES:]

    copies = []
    chunk = out_ref.shape[0] // CHUNKS
    for k in range(CHUNKS):
        part = pl.ds(k * chunk, chunk)
        staged[part, :LANES] = acc0[part, :].astype(bf16)
        staged[part, LANES:] = acc1[part, :].astype(bf16)
        copies.append(pltpu.make_async_copy(staged.at[part, :], out_ref.at[part, :], sems.at[k]))
        copies[-1].start()
    for copy in copies:
        copy.wait()


def right_products(me, values, held, rest, slot_row, slot_col, blocks):
    slots = values.shape[0]
    f32 = jnp.float32
    vmem = pl.BlockSpec(memory_space=pltpu.VMEM)
    return pl.pallas_call(
        right_kernel,
        out_shape=[
            jax.ShapeDtypeStruct((BS * CB, slots), f32),
            jax.ShapeDtypeStruct((1, slots), jnp.int32),
            jax.ShapeDtypeStruct((slots, blocks), jnp.bfloat16),
        ],
        in_specs=[pl.BlockSpec(memory_space=pltpu.SMEM)] + [vmem] * 5,
        out_specs=[vmem] * 3,
        scratch_shapes=[pltpu.VMEM((BS * BS, slots), f32), pltpu.VMEM((WIDE, slots), f32)],
        compiler_params=pltpu.CompilerParams(vmem_limit_bytes=24 * 1024 * 1024),
    )(me, values, held, rest, slot_row, slot_col)


def coarse_tile(live_count, left, pick, z, coarse_col, slot_row, rows, cols):
    slots = z.shape[1]
    f32 = jnp.float32
    vmem = pl.BlockSpec(memory_space=pltpu.VMEM)
    return pl.pallas_call(
        left_kernel,
        out_shape=jax.ShapeDtypeStruct((rows, cols), jnp.bfloat16),
        in_specs=[pl.BlockSpec(memory_space=pltpu.SMEM)] + [vmem] * 5,
        out_specs=pl.BlockSpec(memory_space=pl.ANY),
        scratch_shapes=[
            pltpu.VMEM((WIDE, slots), f32),
            pltpu.VMEM((rows, LANES), f32),
            pltpu.VMEM((rows, LANES), f32),
            pltpu.VMEM((rows, cols), jnp.bfloat16),
            pltpu.SemaphoreType.DMA((CHUNKS,)),
        ],
        compiler_params=pltpu.CompilerParams(vmem_limit_bytes=24 * 1024 * 1024),
    )(live_count, left, pick, z, coarse_col, slot_row)


def payload_kernel(ids_ref, blocks_ref, mine_ref, copies_ref):
    row = lax.broadcasted_iota(jnp.int32, (QD, LANES), 0)
    ids = jnp.zeros((QD, LANES), jnp.float32)
    for t in range(QD):
        ids = jnp.where(row == t, ids_ref[t].astype(jnp.float32), ids)
    whole = jnp.concatenate([blocks_ref[...].astype(jnp.float32), ids], axis=1).astype(jnp.bfloat16)
    mine_ref[0] = whole
    for k in range(copies_ref.shape[0]):
        copies_ref[k] = whole


def payload(blocks, ids, count):
    vmem = pl.BlockSpec(memory_space=pltpu.VMEM)
    return pl.pallas_call(
        payload_kernel,
        out_shape=[
            pltpu.VMEM((1, QD, WIDE), jnp.bfloat16),
            jax.ShapeDtypeStruct((count, QD, WIDE), jnp.bfloat16),
        ],
        in_specs=[pl.BlockSpec(memory_space=pltpu.SMEM), vmem],
        out_specs=[vmem, vmem],
    )(ids, blocks)


def everywhere(block, axis, size, groups=None):
    copies = jnp.broadcast_to(block[None], (size,) + block.shape)
    return lax.all_to_all(copies, axis, 0, 0, axis_index_groups=groups, tiled=True)


def shards(block_values, slot_rows, slot_cols, tile_counts, prolong_blocks, aggregate_ids):
    row_size = lax.axis_size("row")
    col_size = lax.axis_size("col")
    planes = col_size // NEAR
    mine, copies = payload(prolong_blocks, aggregate_ids, planes)
    held = mine
    step = row_size // 2
    while step > 1:
        held = jnp.concatenate([held, lax.ppermute(held, "row", [(r ^ step, r) for r in range(row_size)])], axis=0)
        step //= 2
    rest = lax.ppermute(held, "row", [(r ^ step, r) for r in range(row_size)])
    held = held.reshape(row_size // 2 * QD, WIDE)
    rest = rest.reshape(row_size // 2 * QD, WIDE)
    me = lax.axis_index("row").astype(jnp.int32).reshape(1, 1)
    yz_groups = [[p * NEAR + x for p in range(planes)] for x in range(NEAR)]
    x_groups = [[p * NEAR + x for x in range(NEAR)] for p in range(planes)]
    plane = lax.all_to_all(copies, "col", 0, 0, axis_index_groups=yz_groups, tiled=True).reshape(planes * QD, WIDE)
    plane, held = lax.optimization_barrier((plane, held))
    left = everywhere(plane, "col", NEAR, x_groups).reshape(col_size * QD, WIDE)
    z, coarse_col, pick = right_products(me, block_values, held, rest, slot_rows, slot_cols, col_size * QD)
    return coarse_tile(
        tile_counts, left, pick, z, coarse_col, slot_rows, col_size * AD * CB, row_size * AD * CB
    )


def solution(mesh):
    placed = (
        P("row", "col"),
        P("row", "col"),
        P("row", "col"),
        P("row", "col"),
        P(("row", "col"), None),
        P(("row", "col")),
    )
    return jax.shard_map(
        shards, mesh=mesh, in_specs=placed, out_specs=P("row", "col"), check_vma=False
    )
```

```python
import jax
import jax.numpy as jnp
from jax import lax
from jax.experimental import pallas as pl
from jax.experimental.pallas import tpu as pltpu
from jax.sharding import PartitionSpec as P

BS = 64
CB = 16
AD = 2
QD = 4
NEAR = 4
LANES = 128
PARTS = 2
CHUNKS = 6
WIDE = BS * CB + LANES


def hot_slots(index, blocks):
    slots = index.shape[1]
    hot = lax.broadcasted_iota(jnp.int32, (blocks, slots), 0) == index
    return hot.astype(jnp.float32).T.astype(jnp.bfloat16)


def slots_to_lanes(picked, target):
    for k in range(WIDE // LANES):
        target[pl.ds(k * LANES, LANES), :] = picked[:, k * LANES:(k + 1) * LANES].T


def right_kernel(me_ref, a_ref, held_ref, rest_ref, row_ref, col_ref, z_ref, coarse_ref, pick_ref, at, rt):
    f32 = jnp.float32
    slots = a_ref.shape[0]
    slot_col = col_ref[...]
    half = held_ref.shape[0]
    away = (slot_col >> 2) ^ me_ref[0, 0]
    turned = ((away & 1) << 2) | (away & 2) | (away >> 2)
    place = turned * QD + (slot_col & (QD - 1))
    picked = jnp.dot(hot_slots(place, half), held_ref[...], preferred_element_type=f32)
    picked += jnp.dot(hot_slots(place - half, half), rest_ref[...], preferred_element_type=f32)
    slots_to_lanes(picked, rt)
    for k in range(BS * BS // LANES):
        at[pl.ds(k * LANES, LANES), :] = a_ref[:, k * LANES:(k + 1) * LANES].astype(f32).T

    group = 8

    def x_block(b, carry):
        base = pl.multiple_of(b * (group * BS), group * BS)
        sums = [jnp.zeros((CB, slots), f32) for _ in range(group)]
        for z in range(BS):
            r = rt[pl.ds(z * CB, CB), :]
            for xi in range(group):
                sums[xi] = sums[xi] + at[pl.ds(base + (xi * BS + z), 1), :] * r
        for xi in range(group):
            z_ref[pl.ds(pl.multiple_of(b * (group * CB), group * CB) + xi * CB, CB), :] = sums[xi]
        return carry

    lax.fori_loop(0, BS // group, x_block, 0)
    coarse_ref[...] = (slot_col >> 2) * AD + rt[pl.ds(BS * CB, 1), :].astype(jnp.int32)
    slot_row = row_ref[...]
    device = slot_row >> 2
    blocks = pick_ref.shape[1]
    place = (device & (NEAR - 1)) * (blocks // NEAR) + (device >> 2) * QD + (slot_row & (QD - 1))
    pick_ref[...] = hot_slots(place, blocks)


def left_kernel(count_ref, left_ref, pick_ref, z_ref, coarse_ref, row_ref, out_ref, lt, acc0, acc1, staged, sems):
    f32 = jnp.float32
    bf16 = jnp.bfloat16
    slots = z_ref.shape[1]
    slots_to_lanes(jnp.dot(pick_ref[...], left_ref[...], preferred_element_type=f32), lt)

    def x_step(b, sums):
        base = pl.multiple_of(b * (8 * CB), 8 * CB)
        sums = list(sums)
        for xi in range(8):
            zx = z_ref[pl.ds(base + xi * CB, CB), :]
            for u in range(CB):
                sums[u] = sums[u] + lt[pl.ds(base + (xi * CB + u), 1), :] * zx
        return tuple(sums)

    terms = lax.fori_loop(0, BS // 8, x_step, tuple(jnp.zeros((CB, slots), f32) for _ in range(CB)))

    coarse_row = (row_ref[...] >> 2) * AD + lt[pl.ds(BS * CB, 1), :].astype(jnp.int32)
    live = lax.broadcasted_iota(jnp.int32, (1, slots), 1) < count_ref[0, 0]
    coarse_row = jnp.where(live, coarse_row, -1)
    coarse_col = coarse_ref[...]
    rows = out_ref.shape[0] // CB
    cols = out_ref.shape[1] // CB
    hot = (lax.broadcasted_iota(jnp.int32, (rows, slots), 0) == coarse_row).astype(bf16)
    hot = jnp.concatenate([hot] * PARTS, axis=1)
    masks = [jnp.broadcast_to((coarse_col == v).astype(f32), (CB, slots)).astype(bf16) for v in range(cols)]

    for u in range(CB):
        rest = terms[u]
        placed = []
        for _ in range(PARTS):
            part = rest.astype(bf16)
            rest = rest - part.astype(f32)
            placed.append(jnp.concatenate([mask * part for mask in masks], axis=0))
        placed = jnp.concatenate(placed, axis=1)
        summed = lax.dot_general(hot, placed, (((1,), (1,)), ((), ())), preferred_element_type=f32)
        acc0[pl.ds(u, rows, stride=CB), :] = summed[:, :LANES]
        acc1[pl.ds(u, rows, stride=CB), :] = summed[:, LANES:]

    copies = []
    chunk = out_ref.shape[0] // CHUNKS
    for k in range(CHUNKS):
        part = pl.ds(k * chunk, chunk)
        staged[part, :LANES] = acc0[part, :].astype(bf16)
        staged[part, LANES:] = acc1[part, :].astype(bf16)
        copies.append(pltpu.make_async_copy(staged.at[part, :], out_ref.at[part, :], sems.at[k]))
        copies[-1].start()
    for copy in copies:
        copy.wait()


def right_products(me, values, held, rest, slot_row, slot_col, blocks):
    slots = values.shape[0]
    f32 = jnp.float32
    vmem = pl.BlockSpec(memory_space=pltpu.VMEM)
    return pl.pallas_call(
        right_kernel,
        out_shape=[
            jax.ShapeDtypeStruct((BS * CB, slots), f32),
            jax.ShapeDtypeStruct((1, slots), jnp.int32),
            jax.ShapeDtypeStruct((slots, blocks), jnp.bfloat16),
        ],
        in_specs=[pl.BlockSpec(memory_space=pltpu.SMEM)] + [vmem] * 5,
        out_specs=[vmem] * 3,
        scratch_shapes=[pltpu.VMEM((BS * BS, slots), f32), pltpu.VMEM((WIDE, slots), f32)],
        compiler_params=pltpu.CompilerParams(vmem_limit_bytes=24 * 1024 * 1024),
    )(me, values, held, rest, slot_row, slot_col)


def coarse_tile(live_count, left, pick, z, coarse_col, slot_row, rows, cols):
    slots = z.shape[1]
    f32 = jnp.float32
    vmem = pl.BlockSpec(memory_space=pltpu.VMEM)
    return pl.pallas_call(
        left_kernel,
        out_shape=jax.ShapeDtypeStruct((rows, cols), jnp.bfloat16),
        in_specs=[pl.BlockSpec(memory_space=pltpu.SMEM)] + [vmem] * 5,
        out_specs=pl.BlockSpec(memory_space=pl.ANY),
        scratch_shapes=[
            pltpu.VMEM((WIDE, slots), f32),
            pltpu.VMEM((rows, LANES), f32),
            pltpu.VMEM((rows, LANES), f32),
            pltpu.VMEM((rows, cols), jnp.bfloat16),
            pltpu.SemaphoreType.DMA((CHUNKS,)),
        ],
        compiler_params=pltpu.CompilerParams(vmem_limit_bytes=24 * 1024 * 1024),
    )(live_count, left, pick, z, coarse_col, slot_row)


def payload_kernel(ids_ref, blocks_ref, mine_ref, copies_ref):
    row = lax.broadcasted_iota(jnp.int32, (QD, LANES), 0)
    ids = jnp.zeros((QD, LANES), jnp.float32)
    for t in range(QD):
        ids = jnp.where(row == t, ids_ref[t].astype(jnp.float32), ids)
    whole = jnp.concatenate([blocks_ref[...].astype(jnp.float32), ids], axis=1).astype(jnp.bfloat16)
    mine_ref[0] = whole
    for k in range(copies_ref.shape[0]):
        copies_ref[k] = whole


def payload(blocks, ids, count):
    vmem = pl.BlockSpec(memory_space=pltpu.VMEM)
    return pl.pallas_call(
        payload_kernel,
        out_shape=[
            pltpu.VMEM((1, QD, WIDE), jnp.bfloat16),
            jax.ShapeDtypeStruct((count, QD, WIDE), jnp.bfloat16),
        ],
        in_specs=[pl.BlockSpec(memory_space=pltpu.SMEM), vmem],
        out_specs=[vmem, vmem],
    )(ids, blocks)


def everywhere(block, axis, size, groups=None):
    copies = jnp.broadcast_to(block[None], (size,) + block.shape)
    return lax.all_to_all(copies, axis, 0, 0, axis_index_groups=groups, tiled=True)


def shards(block_values, slot_rows, slot_cols, tile_counts, prolong_blocks, aggregate_ids):
    row_size = lax.axis_size("row")
    col_size = lax.axis_size("col")
    planes = col_size // NEAR
    mine, copies = payload(prolong_blocks, aggregate_ids, planes)
    yz_groups = [[p * NEAR + x for p in range(planes)] for x in range(NEAR)]
    plane = lax.all_to_all(copies, "col", 0, 0, axis_index_groups=yz_groups, tiled=True).reshape(planes * QD, WIDE)
    held = mine
    step = row_size // 2
    while step > 1:
        held = jnp.concatenate([held, lax.ppermute(held, "row", [(r ^ step, r) for r in range(row_size)])], axis=0)
        if step == row_size // 2:
            plane, held = lax.optimization_barrier((plane, held))
        step //= 2
    rest = lax.ppermute(held, "row", [(r ^ step, r) for r in range(row_size)])
    held = held.reshape(row_size // 2 * QD, WIDE)
    rest = rest.reshape(row_size // 2 * QD, WIDE)
    me = lax.axis_index("row").astype(jnp.int32).reshape(1, 1)
    x_groups = [[p * NEAR + x for x in range(NEAR)] for p in range(planes)]
    left = everywhere(plane, "col", NEAR, x_groups).reshape(col_size * QD, WIDE)
    z, coarse_col, pick = right_products(me, block_values, held, rest, slot_rows, slot_cols, col_size * QD)
    return coarse_tile(
        tile_counts, left, pick, z, coarse_col, slot_rows, col_size * AD * CB, row_size * AD * CB
    )


def solution(mesh):
    placed = (
        P("row", "col"),
        P("row", "col"),
        P("row", "col"),
        P("row", "col"),
        P(("row", "col"), None),
        P(("row", "col")),
    )
    return jax.shard_map(
        shards, mesh=mesh, in_specs=placed, out_specs=P("row", "col"), check_vma=False
    )
```
